128 devices in a mesh: fsdp: 64 (over z_lo, y, x, core), rep: 2 (over z_hi).
Axes of the slice: x: 4, y: 4, z: 4 (z_hi: 2, z_lo: 2; z = z_hi * 2 + z_lo), core: 2. Of those that a mesh axis runs over, the one named last changes fastest.
Arguments:
- gate_up: bfloat16 [8, 7168, 4096], P(None, ('fsdp', 'rep')), may hold values from -2 to 2
- expert_owner: int32 [8], replicated, may hold values from 0 to 7, each once
Outputs:
- rollout_weights: bfloat16 [64, 7168, 512], P('fsdp')
- block_scale: float32 [64, 56, 4], P('fsdp')
The draws below stay inside these ranges and needn't reach their ends.
Inputs may be any that keep to these rules, and one draw needn't show every extreme that they name: `expert_owner`: each of the 8 rollout groups owns exactly one expert.
All inputs are finite; a program needn't handle non-finite values. Where the reference program divides by a largest or mean magnitude, that divisor is 1e-20 or more.
Results may differ from the reference program's by a relative error of at most 0.001.
Values may be sent and summed in bfloat16 or wider, within the bound.
No kernel may reach another device: no remote copies, remote signals or barrier semaphores. Data moves between devices by JAX's collectives and lax.ppermute only.
A program may use at most 128 MiB of HBM per device.

```python
import math
import jax
import jax.numpy as jnp
from jax import lax

D = 7168
FF = 2048
GRP = 8
BLOCK = 128
EXPERTS = 8
SHARD = 256


def draw_gate_up(key, part):
    key = jax.random.fold_in(key, 11)
    key_base, key_spread = jax.random.split(key, 2)
    shape = (EXPERTS, D, 2 * FF)
    spread = jnp.exp(jax.random.uniform(key_spread, shape, jnp.float32) * math.log(16.0))
    values = jnp.clip(jax.random.normal(key_base, shape, jnp.float32), -6.0, 6.0) * spread * 0.02
    return values.astype(jnp.bfloat16)


def setup_inputs(seed: int = 0) -> dict:
    key_list = jax.random.split(jax.random.key(seed), 3)
    return {
        "gate_up": draw_gate_up(jax.random.fold_in(key_list[2], 71), 0),
        "expert_owner": jax.random.permutation(key_list[1], EXPERTS).astype(jnp.int32),
    }


epsilon = 1e-6


def reference(gate_up, expert_owner):
    expert_ids = jnp.arange(EXPERTS, dtype=jnp.int32)
    owned = jnp.sum(expert_ids[:, None] * (expert_owner[:, None] == expert_ids[None, :]).astype(jnp.int32), axis=0).astype(jnp.int32)

    def regroup_one(index):
        matrix = lax.dynamic_index_in_dim(gate_up, index, 0, keepdims=False)
        ranked = matrix.reshape(D, 2, GRP, SHARD).transpose(2, 0, 1, 3).reshape(GRP, D, 2 * SHARD)
        blocks = ranked.astype(jnp.float32).reshape(GRP, D // BLOCK, BLOCK, 2 * SHARD // BLOCK, BLOCK)
        peaks = jnp.max(jnp.abs(blocks), axis=(2, 4))
        scaled = (blocks / (peaks[:, :, None, :, None] + epsilon)).astype(jnp.bfloat16)
        return scaled.reshape(GRP, D, 2 * SHARD), peaks

    scaled, peaks = lax.map(regroup_one, owned)
    return scaled.reshape(EXPERTS * GRP, D, 2 * SHARD), peaks.reshape(EXPERTS * GRP, D // BLOCK, 2 * SHARD // BLOCK)
```

```python
import jax
import jax.numpy as jnp
from jax import lax
from jax.experimental import pallas as pl
from jax.experimental.pallas import tpu as pltpu
from jax.sharding import PartitionSpec as P

GRP = 8
BLOCK = 128
BANDS = 8

epsilon = 1e-06


def arrange_kernel(owned_ref, x_ref, o_ref):
    del owned_ref
    shard = x_ref.shape[2] // 2 // GRP
    copies = o_ref.shape[0] // GRP
    for j in range(GRP):
        for half in range(2):
            part = x_ref[0, :, pl.ds((half * GRP + j) * shard, shard)]
            for r in range(copies):
                o_ref[j * copies + r, :, pl.ds(half * shard, shard)] = part


def arrange(owned, gate_up, copies):
    experts, rows, width = gate_up.shape
    columns = width // GRP
    return pl.pallas_call(
        arrange_kernel,
        out_shape=jax.ShapeDtypeStruct((experts * GRP * copies, rows, columns), gate_up.dtype),
        grid_spec=pltpu.PrefetchScalarGridSpec(
            num_scalar_prefetch=1,
            grid=(experts,),
            in_specs=[pl.BlockSpec((1, rows, width), lambda g, owned: (owned[g], 0, 0))],
            out_specs=pl.BlockSpec((GRP * copies, rows, columns), lambda g, owned: (g, 0, 0)),
        ),
        compiler_params=pltpu.CompilerParams(vmem_limit_bytes=32 * 2**20),
        name="arrange",
    )(owned, gate_up)


def scale_kernel(x_ref, o_ref, s_ref):
    columns = x_ref.shape[1]
    for b in range(BANDS):
        rows = pl.ds(b * BLOCK, BLOCK)
        peaks = []
        for c in range(columns // BLOCK):
            lanes = pl.ds(c * BLOCK, BLOCK)
            x = x_ref[rows, lanes]
            top = jnp.max(jnp.abs(x).astype(jnp.float32), axis=0, keepdims=True)
            peak = jnp.max(top, axis=1, keepdims=True)
            inverse = 1.0 / (peak + epsilon)
            o_ref[rows, lanes] = (x.astype(jnp.float32) * inverse).astype(o_ref.dtype)
            peaks.append(peak)
        s_ref[b : b + 1, :] = jnp.concatenate(peaks, axis=1)


def scale_blocks(x):
    rows, columns = x.shape
    step = BANDS * BLOCK
    return pl.pallas_call(
        scale_kernel,
        out_shape=(
            jax.ShapeDtypeStruct((rows, columns), x.dtype),
            jax.ShapeDtypeStruct((rows // BLOCK, columns // BLOCK), jnp.float32),
        ),
        grid=(rows // step,),
        in_specs=[pl.BlockSpec((step, columns), lambda i: (i, 0))],
        out_specs=(
            pl.BlockSpec((step, columns), lambda i: (i, 0)),
            pl.BlockSpec((BANDS, columns // BLOCK), lambda i: (i, 0)),
        ),
        compiler_params=pltpu.CompilerParams(vmem_limit_bytes=32 * 2**20),
        name="scale_blocks",
    )(x)


def on_device(gate_up, expert_owner):
    experts, rows_dev, width = gate_up.shape
    columns = width // GRP
    devices = lax.axis_size(("fsdp", "rep"))
    expert_ids = jnp.arange(experts, dtype=jnp.int32)
    owned = jnp.sum(
        expert_ids[:, None] * (expert_owner[:, None] == expert_ids[None, :]).astype(jnp.int32),
        axis=0,
    )
    outgoing = arrange(owned, gate_up, lax.axis_size("rep"))
    received = lax.all_to_all(outgoing, ("fsdp", "rep"), split_axis=0, concat_axis=0, tiled=True)
    whole, peaks = scale_blocks(received.reshape(devices * rows_dev, columns))
    return (whole[None], peaks[None])


def solution(mesh):
    placed = (P(None, ("fsdp", "rep"), None), P())
    return jax.shard_map(
        on_device,
        mesh=mesh,
        in_specs=placed,
        out_specs=(P("fsdp", None, None), P("fsdp", None, None)),
        check_vma=False,
    )
```

```python
import jax
import jax.numpy as jnp
from jax import lax
from jax.experimental import pallas as pl
from jax.experimental.pallas import tpu as pltpu
from jax.sharding import PartitionSpec as P

GRP = 8
BLOCK = 128
BANDS = 8

epsilon = 1e-06


def arrange_kernel(owner_ref, x_ref, o_ref):
    experts = x_ref.shape[0]
    shard = x_ref.shape[2] // 2 // GRP
    copies = o_ref.shape[0] // GRP // experts

    def regroup(g, carry):
        expert = jnp.int32(0)
        for e in range(experts):
            expert = expert + jnp.where(owner_ref[e] == g, e, 0)
        for j in range(GRP):
            for half in range(2):
                part = x_ref[expert, :, pl.ds((half * GRP + j) * shard, shard)]
                for r in range(copies):
                    o_ref[(g * GRP + j) * copies + r, :, pl.ds(half * shard, shard)] = part
        return carry

    lax.fori_loop(0, experts, regroup, 0)


def arrange(expert_owner, gate_up, copies):
    experts, rows, width = gate_up.shape
    columns = width // GRP
    return pl.pallas_call(
        arrange_kernel,
        out_shape=jax.ShapeDtypeStruct((experts * GRP * copies, rows, columns), gate_up.dtype),
        in_specs=[
            pl.BlockSpec(memory_space=pltpu.SMEM),
            pl.BlockSpec(memory_space=pltpu.VMEM),
        ],
        out_specs=pl.BlockSpec(memory_space=pltpu.VMEM),
        compiler_params=pltpu.CompilerParams(vmem_limit_bytes=32 * 2**20),
        name="arrange",
    )(expert_owner, gate_up)


def scale_kernel(x_ref, o_ref, s_ref, scaled, peaks_ref, sems):
    rows, columns = x_ref.shape
    step = BANDS * BLOCK
    steps = rows // step

    def copy_out(i):
        part = pl.ds(pl.multiple_of(i * step, step), step)
        return pltpu.make_async_copy(scaled.at[part], o_ref.at[part], sems.at[i])

    def scale_step(i, carry):
        start = pl.multiple_of(i * step, step)
        tops = []
        for b in range(BANDS):
            top = jnp.abs(x_ref[pl.ds(start + b * BLOCK, 16), :])
            for r in range(16, BLOCK, 16):
                top = jnp.maximum(top, jnp.abs(x_ref[pl.ds(start + b * BLOCK + r, 16), :]))
            tops.append(jnp.max(top.astype(jnp.float32), axis=0, keepdims=True))
        tops = jnp.concatenate(tops, axis=0)

        peaks = []
        for c in range(columns // BLOCK):
            lanes = pl.ds(c * BLOCK, BLOCK)
            peak = jnp.max(tops[:, c * BLOCK : (c + 1) * BLOCK], axis=1, keepdims=True)
            inverse = 1.0 / (peak + epsilon)
            for b in range(BANDS):
                band = pl.ds(start + b * BLOCK, BLOCK)
                scaled[band, lanes] = (x_ref[band, lanes].astype(jnp.float32) * inverse[b : b + 1]).astype(scaled.dtype)
            peaks.append(peak)
        copy_out(i).start()
        peaks_ref[pl.ds(pl.multiple_of(i * BANDS, BANDS), BANDS), : columns // BLOCK] = jnp.concatenate(peaks, axis=1)
        return carry

    lax.fori_loop(0, steps, scale_step, 0)
    s_ref[...] = peaks_ref[...].T[: s_ref.shape[0], : s_ref.shape[1]]
    for i in range(steps):
        copy_out(i).wait()


def scale_blocks(x):
    rows, columns = x.shape
    return pl.pallas_call(
        scale_kernel,
        out_shape=(
            jax.ShapeDtypeStruct((rows, columns), x.dtype),
            jax.ShapeDtypeStruct((columns // BLOCK, rows // BLOCK), jnp.float32),
        ),
        in_specs=[pl.BlockSpec(memory_space=pltpu.VMEM)],
        out_specs=(
            pl.BlockSpec(memory_space=pl.ANY),
            pl.BlockSpec(memory_space=pltpu.VMEM),
        ),
        scratch_shapes=[
            pltpu.VMEM((rows, columns), x.dtype),
            pltpu.VMEM((BLOCK, BLOCK), jnp.float32),
            pltpu.SemaphoreType.DMA((rows // (BANDS * BLOCK),)),
        ],
        compiler_params=pltpu.CompilerParams(vmem_limit_bytes=32 * 2**20),
        name="scale_blocks",
    )(x)


def on_device(gate_up, expert_owner):
    rows_dev, width = gate_up.shape[1:]
    devices = lax.axis_size(("fsdp", "rep"))
    outgoing = arrange(expert_owner, gate_up, lax.axis_size("rep"))
    received = lax.all_to_all(outgoing, ("fsdp", "rep"), split_axis=0, concat_axis=0, tiled=True)
    whole, peaks = scale_blocks(received.reshape(devices * rows_dev, width // GRP))
    return (whole[None], peaks.T[None])


def solution(mesh):
    placed = (P(None, ("fsdp", "rep"), None), P())
    return jax.shard_map(
        on_device,
        mesh=mesh,
        in_specs=placed,
        out_specs=(P("fsdp", None, None), P("fsdp", None, None)),
        check_vma=False,
    )
```

```python
import jax
import jax.numpy as jnp
from jax import lax
from jax.experimental import pallas as pl
from jax.experimental.pallas import tpu as pltpu
from jax.sharding import PartitionSpec as P

GRP = 8
BLOCK = 128
BANDS = 8

epsilon = 1e-06


def arrange_kernel(owner_ref, x_ref, o_ref, buf, sems):
    experts = x_ref.shape[0]
    shard = x_ref.shape[2] // 2 // GRP
    copies = o_ref.shape[0] // GRP // experts

    def fetch(g):
        expert = jnp.int32(0)
        for e in range(experts):
            expert = expert + jnp.where(owner_ref[e] == g, e, 0)
        return pltpu.make_async_copy(x_ref.at[expert], buf.at[g], sems.at[g])

    for g in range(experts):
        fetch(g).start()

    def regroup(g, carry):
        pltpu.make_async_copy(x_ref.at[0], buf.at[g], sems.at[g]).wait()
        for j in range(GRP):
            for half in range(2):
                part = buf[g, :, pl.ds((half * GRP + j) * shard, shard)]
                for r in range(copies):
                    o_ref[(g * GRP + j) * copies + r, :, pl.ds(half * shard, shard)] = part
        return carry

    lax.fori_loop(0, experts, regroup, 0)


def arrange(expert_owner, gate_up, copies):
    experts, rows, width = gate_up.shape
    columns = width // GRP
    return pl.pallas_call(
        arrange_kernel,
        out_shape=jax.ShapeDtypeStruct((experts * GRP * copies, rows, columns), gate_up.dtype),
        in_specs=[
            pl.BlockSpec(memory_space=pltpu.SMEM),
            pl.BlockSpec(memory_space=pltpu.HBM),
        ],
        out_specs=pl.BlockSpec(memory_space=pltpu.VMEM),
        scratch_shapes=[
            pltpu.VMEM(gate_up.shape, gate_up.dtype),
            pltpu.SemaphoreType.DMA((experts,)),
        ],
        compiler_params=pltpu.CompilerParams(vmem_limit_bytes=32 * 2**20),
        name="arrange",
    )(
        pltpu.with_memory_space_constraint(expert_owner, pltpu.HBM),
        pltpu.with_memory_space_constraint(gate_up, pltpu.HBM),
    )


def scale_kernel(x_ref, o_ref, s_ref, scaled, peaks_ref, sems):
    rows, columns = x_ref.shape
    step = BANDS * BLOCK
    steps = rows // step

    def copy_out(i):
        part = pl.ds(pl.multiple_of(i * step, step), step)
        return pltpu.make_async_copy(scaled.at[part], o_ref.at[part], sems.at[i])

    def scale_step(i, carry):
        start = pl.multiple_of(i * step, step)
        tops = []
        for b in range(BANDS):
            top = jnp.abs(x_ref[pl.ds(start + b * BLOCK, 16), :])
            for r in range(16, BLOCK, 16):
                top = jnp.maximum(top, jnp.abs(x_ref[pl.ds(start + b * BLOCK + r, 16), :]))
            tops.append(jnp.max(top.astype(jnp.float32), axis=0, keepdims=True))
        tops = jnp.concatenate(tops, axis=0)

        peaks = []
        for c in range(columns // BLOCK):
            lanes = pl.ds(c * BLOCK, BLOCK)
            peak = jnp.max(tops[:, c * BLOCK : (c + 1) * BLOCK], axis=1, keepdims=True)
            inverse = 1.0 / (peak + epsilon)
            for b in range(BANDS):
                band = pl.ds(start + b * BLOCK, BLOCK)
                scaled[band, lanes] = (x_ref[band, lanes].astype(jnp.float32) * inverse[b : b + 1]).astype(scaled.dtype)
            peaks.append(peak)
        copy_out(i).start()
        peaks_ref[pl.ds(pl.multiple_of(i * BANDS, BANDS), BANDS), : columns // BLOCK] = jnp.concatenate(peaks, axis=1)
        return carry

    lax.fori_loop(0, steps, scale_step, 0)
    s_ref[...] = peaks_ref[...].T[: s_ref.shape[0], : s_ref.shape[1]]
    for i in range(steps):
        copy_out(i).wait()


def scale_blocks(x):
    rows, columns = x.shape
    return pl.pallas_call(
        scale_kernel,
        out_shape=(
            jax.ShapeDtypeStruct((rows, columns), x.dtype),
            jax.ShapeDtypeStruct((columns // BLOCK, rows // BLOCK), jnp.float32),
        ),
        in_specs=[pl.BlockSpec(memory_space=pltpu.VMEM)],
        out_specs=(
            pl.BlockSpec(memory_space=pl.ANY),
            pl.BlockSpec(memory_space=pltpu.VMEM),
        ),
        scratch_shapes=[
            pltpu.VMEM((rows, columns), x.dtype),
            pltpu.VMEM((BLOCK, BLOCK), jnp.float32),
            pltpu.SemaphoreType.DMA((rows // (BANDS * BLOCK),)),
        ],
        compiler_params=pltpu.CompilerParams(vmem_limit_bytes=32 * 2**20),
        name="scale_blocks",
    )(x)


def on_device(gate_up, expert_owner):
    rows_dev, width = gate_up.shape[1:]
    devices = lax.axis_size(("fsdp", "rep"))
    outgoing = arrange(expert_owner, gate_up, lax.axis_size("rep"))
    received = lax.all_to_all(outgoing, ("fsdp", "rep"), split_axis=0, concat_axis=0, tiled=True)
    whole, peaks = scale_blocks(received.reshape(devices * rows_dev, width // GRP))
    return (whole[None], peaks.T[None])


def solution(mesh):
    placed = (P(None, ("fsdp", "rep"), None), P())
    return jax.shard_map(
        on_device,
        mesh=mesh,
        in_specs=placed,
        out_specs=(P("fsdp", None, None), P("fsdp", None, None)),
        check_vma=False,
    )
```

```python
import jax
import jax.numpy as jnp
from jax import lax
from jax.experimental import pallas as pl
from jax.experimental.pallas import tpu as pltpu
from jax.sharding import PartitionSpec as P

GRP = 8
BLOCK = 128
BANDS = 8

epsilon = 1e-06


def arrange_kernel(owner_hbm, x_ref, o_ref, owner_ref, buf, owner_sem, sems):
    experts = x_ref.shape[0]
    shard = x_ref.shape[2] // 2 // GRP
    copies = o_ref.shape[0] // GRP // experts

    def fetch(e):
        return pltpu.make_async_copy(x_ref.at[e], buf.at[e], sems.at[e])

    owners = pltpu.make_async_copy(owner_hbm, owner_ref, owner_sem)
    owners.start()
    for e in range(experts):
        fetch(e).start()
    owners.wait()

    def regroup(e, carry):
        fetch(e).wait()
        first = owner_ref[e] * (GRP * copies)
        for j in range(GRP):
            for half in range(2):
                part = buf[e, :, pl.ds((half * GRP + j) * shard, shard)]
                for r in range(copies):
                    o_ref[first + (j * copies + r), :, pl.ds(half * shard, shard)] = part
        return carry

    lax.fori_loop(0, experts, regroup, 0)


def arrange(expert_owner, gate_up, copies):
    experts, rows, width = gate_up.shape
    columns = width // GRP
    return pl.pallas_call(
        arrange_kernel,
        out_shape=jax.ShapeDtypeStruct((experts * GRP * copies, rows, columns), gate_up.dtype),
        in_specs=[
            pl.BlockSpec(memory_space=pltpu.HBM),
            pl.BlockSpec(memory_space=pltpu.HBM),
        ],
        out_specs=pl.BlockSpec(memory_space=pltpu.VMEM),
        scratch_shapes=[
            pltpu.SMEM(expert_owner.shape, expert_owner.dtype),
            pltpu.VMEM(gate_up.shape, gate_up.dtype),
            pltpu.SemaphoreType.DMA,
            pltpu.SemaphoreType.DMA((experts,)),
        ],
        compiler_params=pltpu.CompilerParams(vmem_limit_bytes=32 * 2**20),
        name="arrange",
    )(
        pltpu.with_memory_space_constraint(expert_owner, pltpu.HBM),
        pltpu.with_memory_space_constraint(gate_up, pltpu.HBM),
    )


def scale_kernel(x_ref, o_ref, s_ref, scaled, peaks_ref, sems):
    rows, columns = x_ref.shape
    step = BANDS * BLOCK
    steps = rows // step

    def copy_out(i):
        part = pl.ds(pl.multiple_of(i * step, step), step)
        return pltpu.make_async_copy(scaled.at[part], o_ref.at[part], sems.at[i])

    def find_peaks(i):
        start = pl.multiple_of(i * step, step)
        tops = []
        for b in range(BANDS):
            top = jnp.abs(x_ref[pl.ds(start + b * BLOCK, 16), :])
            for r in range(16, BLOCK, 16):
                top = jnp.maximum(top, jnp.abs(x_ref[pl.ds(start + b * BLOCK + r, 16), :]))
            tops.append(jnp.max(top.astype(jnp.float32), axis=0, keepdims=True))
        tops = jnp.concatenate(tops, axis=0)
        peaks = [
            jnp.max(tops[:, c * BLOCK : (c + 1) * BLOCK], axis=1, keepdims=True)
            for c in range(columns // BLOCK)
        ]
        peaks_ref[pl.ds(pl.multiple_of(i * BANDS, BANDS), BANDS), : columns // BLOCK] = jnp.concatenate(peaks, axis=1)
        return tuple(1.0 / (peak + epsilon) for peak in peaks)

    def scale_step(i, inverses):
        start = pl.multiple_of(i * step, step)
        later = find_peaks(jnp.minimum(i + 1, steps - 1))
        for b in range(BANDS):
            band = pl.ds(start + b * BLOCK, BLOCK)
            for c, inverse in enumerate(inverses):
                lanes = pl.ds(c * BLOCK, BLOCK)
                scaled[band, lanes] = (x_ref[band, lanes].astype(jnp.float32) * inverse[b : b + 1]).astype(scaled.dtype)
        copy_out(i).start()
        return later

    lax.fori_loop(0, steps, scale_step, find_peaks(0))
    s_ref[...] = peaks_ref[...].T[: s_ref.shape[0], : s_ref.shape[1]]
    for i in range(steps):
        copy_out(i).wait()


def scale_blocks(x):
    rows, columns = x.shape
    return pl.pallas_call(
        scale_kernel,
        out_shape=(
            jax.ShapeDtypeStruct((rows, columns), x.dtype),
            jax.ShapeDtypeStruct((columns // BLOCK, rows // BLOCK), jnp.float32),
        ),
        in_specs=[pl.BlockSpec(memory_space=pltpu.VMEM)],
        out_specs=(
            pl.BlockSpec(memory_space=pl.ANY),
            pl.BlockSpec(memory_space=pltpu.VMEM),
        ),
        scratch_shapes=[
            pltpu.VMEM((rows, columns), x.dtype),
            pltpu.VMEM((BLOCK, BLOCK), jnp.float32),
            pltpu.SemaphoreType.DMA((rows // (BANDS * BLOCK),)),
        ],
        compiler_params=pltpu.CompilerParams(vmem_limit_bytes=32 * 2**20),
        name="scale_blocks",
    )(x)


def on_device(gate_up, expert_owner):
    rows_dev, width = gate_up.shape[1:]
    devices = lax.axis_size(("fsdp", "rep"))
    outgoing = arrange(expert_owner, gate_up, lax.axis_size("rep"))
    received = lax.all_to_all(outgoing, ("fsdp", "rep"), split_axis=0, concat_axis=0, tiled=True)
    whole, peaks = scale_blocks(received.reshape(devices * rows_dev, width // GRP))
    return (whole[None], peaks.T[None])


def solution(mesh):
    placed = (P(None, ("fsdp", "rep"), None), P())
    return jax.shard_map(
        on_device,
        mesh=mesh,
        in_specs=placed,
        out_specs=(P("fsdp", None, None), P("fsdp", None, None)),
        check_vma=False,
    )
```

```python
import jax
import jax.numpy as jnp
from jax import lax
from jax.experimental import pallas as pl
from jax.experimental.pallas import tpu as pltpu
from jax.sharding import PartitionSpec as P

GRP = 8
BLOCK = 128
BANDS = 8
PART = 4

epsilon = 1e-06


def arrange_kernel(owner_hbm, x_ref, o_ref, owner_ref, buf, owner_sem, sems):
    experts = x_ref.shape[0]
    shard = x_ref.shape[2] // 2 // GRP
    copies = o_ref.shape[0] // GRP // experts

    def fetch(e):
        return pltpu.make_async_copy(x_ref.at[e], buf.at[e], sems.at[e])

    owners = pltpu.make_async_copy(owner_hbm, owner_ref, owner_sem)
    owners.start()
    for e in range(experts):
        fetch(e).start()
    owners.wait()

    def regroup(e, carry):
        fetch(e).wait()
        first = owner_ref[e] * (GRP * copies)
        for j in range(GRP):
            for half in range(2):
                part = buf[e, :, pl.ds((half * GRP + j) * shard, shard)]
                for r in range(copies):
                    o_ref[first + (j * copies + r), :, pl.ds(half * shard, shard)] = part
        return carry

    lax.fori_loop(0, experts, regroup, 0)


def arrange(expert_owner, gate_up, copies):
    experts, rows, width = gate_up.shape
    columns = width // GRP
    return pl.pallas_call(
        arrange_kernel,
        out_shape=jax.ShapeDtypeStruct((experts * GRP * copies, rows, columns), gate_up.dtype),
        in_specs=[
            pl.BlockSpec(memory_space=pltpu.HBM),
            pl.BlockSpec(memory_space=pltpu.HBM),
        ],
        out_specs=pl.BlockSpec(memory_space=pltpu.VMEM),
        scratch_shapes=[
            pltpu.SMEM(expert_owner.shape, expert_owner.dtype),
            pltpu.VMEM(gate_up.shape, gate_up.dtype),
            pltpu.SemaphoreType.DMA,
            pltpu.SemaphoreType.DMA((experts,)),
        ],
        compiler_params=pltpu.CompilerParams(vmem_limit_bytes=32 * 2**20),
        name="arrange",
    )(
        pltpu.with_memory_space_constraint(expert_owner, pltpu.HBM),
        pltpu.with_memory_space_constraint(gate_up, pltpu.HBM),
    )


def scale_kernel(x_ref, o_ref, s_ref, scaled, peaks_ref, table_ref, sems, table_sem):
    rows, columns = x_ref.shape
    step = BANDS * BLOCK
    steps = rows // step

    def copy_out(n):
        part = pl.ds(pl.multiple_of(n * (PART * BLOCK), PART * BLOCK), PART * BLOCK)
        return pltpu.make_async_copy(scaled.at[part], o_ref.at[part], sems.at[n])

    def find_peaks(i):
        start = pl.multiple_of(i * step, step)
        tops = []
        for b in range(BANDS):
            top = jnp.abs(x_ref[pl.ds(start + b * BLOCK, 16), :])
            for r in range(16, BLOCK, 16):
                top = jnp.maximum(top, jnp.abs(x_ref[pl.ds(start + b * BLOCK + r, 16), :]))
            tops.append(jnp.max(top.astype(jnp.float32), axis=0, keepdims=True))
        tops = jnp.concatenate(tops, axis=0)
        peaks = [
            jnp.max(tops[:, c * BLOCK : (c + 1) * BLOCK], axis=1, keepdims=True)
            for c in range(columns // BLOCK)
        ]
        peaks_ref[i, :, : columns // BLOCK] = jnp.concatenate(peaks, axis=1)
        return tuple(1.0 / (peak + epsilon) for peak in peaks)

    def scale_step(i, inverses):
        start = pl.multiple_of(i * step, step)
        later = find_peaks(jnp.minimum(i + 1, steps - 1))
        for b in range(BANDS):
            band = pl.ds(start + b * BLOCK, BLOCK)
            for c, inverse in enumerate(inverses):
                lanes = pl.ds(c * BLOCK, BLOCK)
                scaled[band, lanes] = (x_ref[band, lanes].astype(jnp.float32) * inverse[b : b + 1]).astype(scaled.dtype)
            if b % PART == PART - 1:
                copy_out(i * (BANDS // PART) + b // PART).start()
        return later

    lax.fori_loop(0, steps, scale_step, find_peaks(0))
    table = [peaks_ref[i] for i in range(steps)] + [jnp.zeros((BLOCK - steps * BANDS, BLOCK), jnp.float32)]
    table_ref[...] = jnp.concatenate(table, axis=0).T[: s_ref.shape[0], : s_ref.shape[1]]
    table_out = pltpu.make_async_copy(table_ref, s_ref, table_sem)
    table_out.start()

    def finish(n, carry):
        copy_out(n).wait()
        return carry

    lax.fori_loop(0, rows // (PART * BLOCK), finish, 0)
    table_out.wait()


def scale_blocks(x):
    rows, columns = x.shape
    bands, blocks = rows // BLOCK, columns // BLOCK
    return pl.pallas_call(
        scale_kernel,
        out_shape=(
            jax.ShapeDtypeStruct((rows, columns), x.dtype),
            jax.ShapeDtypeStruct((blocks, bands), jnp.float32),
        ),
        in_specs=[pl.BlockSpec(memory_space=pltpu.VMEM)],
        out_specs=(
            pl.BlockSpec(memory_space=pl.ANY),
            pl.BlockSpec(memory_space=pl.ANY),
        ),
        scratch_shapes=[
            pltpu.VMEM((rows, columns), x.dtype),
            pltpu.VMEM((bands // BANDS, BANDS, BLOCK), jnp.float32),
            pltpu.VMEM((blocks, bands), jnp.float32),
            pltpu.SemaphoreType.DMA((bands // PART,)),
            pltpu.SemaphoreType.DMA,
        ],
        compiler_params=pltpu.CompilerParams(vmem_limit_bytes=32 * 2**20),
        name="scale_blocks",
    )(x)


def on_device(gate_up, expert_owner):
    rows_dev, width = gate_up.shape[1:]
    devices = lax.axis_size(("fsdp", "rep"))
    outgoing = arrange(expert_owner, gate_up, lax.axis_size("rep"))
    received = lax.all_to_all(outgoing, ("fsdp", "rep"), split_axis=0, concat_axis=0, tiled=True)
    whole, peaks = scale_blocks(received.reshape(devices * rows_dev, width // GRP))
    return (whole[None], peaks.T[None])


def solution(mesh):
    placed = (P(None, ("fsdp", "rep"), None), P())
    return jax.shard_map(
        on_device,
        mesh=mesh,
        in_specs=placed,
        out_specs=(P("fsdp", None, None), P("fsdp", None, None)),
        check_vma=False,
    )
```
